512 devices in a mesh: group: 2 (over core), row: 16 (over z_hi, y), col: 16 (over x, z_lo).
Axes of the slice: x: 4, y: 4, z: 16 (z_hi: 4, z_lo: 4; z = z_hi * 4 + z_lo), core: 2. Of those that a mesh axis runs over, the one named last changes fastest.
Arguments:
- activations: bfloat16 [4096, 5120], P(('group', 'col'), 'row'), may hold values from -6 to 6
- cotangent: bfloat16 [4096, 5120], P(('group', 'row'), 'col'), may hold values from -6 to 6
- statistics: float32 [2, 5120, 5120], P('group', 'row', 'col'), as said below
Outputs:
- new_statistics: float32 [2, 5120, 5120], P('group', 'row', 'col')
- roots: bfloat16 [2, 5120, 5120], P('group', 'row', 'col')
- update: bfloat16 [5120, 5120], P('row', 'col')
The draws below stay inside these ranges and needn't reach their ends.
Inputs may be any that keep to these rules, and one draw needn't show every extreme that they name: `statistics`: each of the two matrices is symmetric and positive definite.
All inputs are finite; a program needn't handle non-finite values.
Results may differ from the reference program's by a relative error of at most 0.028.
Values may be sent and summed in bfloat16 or wider, within the bound.
A program may use at most 64 MiB of HBM per device.

```python
import math
import jax
import jax.numpy as jnp
from jax import lax

D = 5120
TOKENS = 4096


def token_gain(key):
    uniform_part = jax.random.uniform(key, (TOKENS,), jnp.float32, -1.0, 1.0)
    position = jnp.arange(TOKENS, dtype=jnp.float32) / TOKENS
    level = jnp.clip(uniform_part + position - 0.5, -1.0, 1.0)
    return jnp.exp(level * math.log(2.0))


def draw_activations(key, part):
    gain = token_gain(key)
    key = jax.random.fold_in(key, 11)
    values = jnp.clip(jax.random.normal(key, (TOKENS, D), jnp.float32), -3.0, 3.0)
    return (gain[:, None] * values).astype(jnp.bfloat16)


def draw_cotangent(key, part):
    gain = token_gain(key)
    key = jax.random.fold_in(key, 13)
    values = jnp.clip(jax.random.normal(key, (TOKENS, D), jnp.float32), -3.0, 3.0)
    feature_place = jnp.arange(D, dtype=jnp.float32) / D
    feature_scale = jnp.exp((2.0 * feature_place - 1.0) * math.log(2.0))
    scaled = gain[:, None] * feature_scale[None, :] * values
    return jnp.clip(scaled, -6.0, 6.0).astype(jnp.bfloat16)


def draw_statistics(key, part):
    key = jax.random.fold_in(key, 7)
    first_key, second_key, third_key = jax.random.split(key, 3)
    position = jnp.arange(D, dtype=jnp.float32) / D
    rough = jnp.exp(0.3 * jax.random.uniform(first_key, (2, D), jnp.float32, -1.0, 1.0))
    spread = math.log(10.0)
    side_scale = jnp.exp(0.5 * spread * position)[None, :] * rough
    noise = jax.random.uniform(second_key, (2, D, D), jnp.float32, -1.0, 1.0) / D
    mirrored = 0.5 * (noise + jnp.swapaxes(noise, 1, 2))
    inner = D // 16
    factors = jax.random.normal(third_key, (2, D, inner), jnp.float32)
    shared = jnp.einsum('kir,kjr->kij', factors, factors, precision=lax.Precision.HIGHEST) / inner
    identity = jnp.eye(D, dtype=jnp.float32)
    core = 0.2 * (identity[None] + 0.5 * mirrored) + 0.7 * shared
    return 0.25 * side_scale[:, :, None] * side_scale[:, None, :] * core


def setup_inputs(seed: int = 0) -> dict:
    keys = jax.random.split(jax.random.key(seed), 4)
    return {
        "activations": draw_activations(jax.random.fold_in(keys[3], 71), 0),
        "cotangent": draw_cotangent(jax.random.fold_in(keys[3], 71), 0),
        "statistics": draw_statistics(jax.random.fold_in(keys[3], 71), 0),
    }


def reference(activations, cotangent, statistics):
    gradient = (jnp.dot(activations.T, cotangent, preferred_element_type=jnp.float32) / math.sqrt(TOKENS)).astype(jnp.bfloat16)
    left_gram = jnp.dot(gradient, gradient.T, preferred_element_type=jnp.float32) / D
    right_gram = jnp.dot(gradient.T, gradient, preferred_element_type=jnp.float32) / D
    new_stats = 0.9 * statistics + jnp.stack([left_gram, right_gram])
    identity = jnp.eye(D, dtype=jnp.float32)
    trace_scale = jnp.trace(new_stats, axis1=1, axis2=2) / D
    factor = trace_scale[:, None, None]
    root_pair = (factor ** (-0.25) * (5.0 * identity - new_stats / factor) / 4.0).astype(jnp.bfloat16)
    left_side = jnp.dot(root_pair[0], gradient, preferred_element_type=jnp.float32).astype(jnp.bfloat16)
    update = jnp.dot(left_side, root_pair[1], preferred_element_type=jnp.float32).astype(jnp.bfloat16)
    return (new_stats, root_pair, update)
```

```python
import jax
import jax.numpy as jnp
from jax import lax
from jax.experimental import pallas as pl
from jax.experimental.pallas import tpu as pltpu
from jax.sharding import PartitionSpec as P

D = 5120
TOKENS = 4096
MESH = pl.DeviceIdType.MESH
F32 = jnp.float32
BF16 = jnp.bfloat16


def kernel(
    acts, cot, stats, new_stats, roots, update,
    a1, b1, a2, b2, p3, p4, part, part_in, gt_out, gt_in, tr, up_in,
    send_sems, recv_sems, tr_send, tr_recv, pair_send, pair_recv, swap_sems,
):
    g = lax.axis_index("group")
    row = lax.axis_index("row")
    col = lax.axis_index("col")
    zh, y = row // 4, row % 4
    x, zl = col // 4, col % 4
    tile = stats.shape[1]
    toks = acts.shape[0]

    def dev_zl(j):
        return (g, row, 4 * x + (zl + j) % 4)

    def dev_x(j):
        return (g, row, 4 * ((x + j) % 4) + zl)

    def dev_zh(j):
        return (g, 4 * ((zh + j) % 4) + y, col)

    def dev_y(j):
        return (g, 4 * zh + (y + j) % 4, col)

    partner = (1 - g, row, col)
    mirror = (g, col, row)
    off = row != col

    barrier = pltpu.get_barrier_semaphore()
    for dev in (dev_zl, dev_x, dev_zh, dev_y):
        for j in (1, 2, 3):
            pl.semaphore_signal(barrier, inc=1, device_id=dev(j), device_id_type=MESH)
    pl.semaphore_signal(barrier, inc=1, device_id=partner, device_id_type=MESH)

    @pl.when(off)
    def _():
        pl.semaphore_signal(barrier, inc=1, device_id=mirror, device_id_type=MESH)
        pl.semaphore_wait(barrier, 14)

    @pl.when(jnp.logical_not(off))
    def _():
        pl.semaphore_wait(barrier, 13)

    def col_axis():
        me = col
        near = lambda j: (dev_zl(j), 4 * x + (zl + j) % 4)
        far = lambda j: (dev_x(j), 4 * ((x + j) % 4) + zl)
        arrive = lambda i, j: 4 * ((x + j) % 4) + (zl + i) % 4
        return me, near, far, arrive

    def row_axis():
        me = row
        near = lambda j: (dev_zh(j), 4 * ((zh + j) % 4) + y)
        far = lambda j: (dev_y(j), 4 * zh + (y + j) % 4)
        arrive = lambda i, j: 4 * ((zh + i) % 4) + (y + j) % 4
        return me, near, far, arrive

    class Gather:
        def __init__(self, n, axis, at):
            self.n, self.at = n, at
            self.me, self.near, self.far, self.arrive = axis
            self.sent = []

        def send(self, slot, device):
            copy = pltpu.make_async_remote_copy(
                src_ref=self.at(slot), dst_ref=self.at(slot),
                send_sem=send_sems.at[self.n, len(self.sent)],
                recv_sem=recv_sems.at[self.n, slot],
                device_id=device, device_id_type=MESH)
            copy.start()
            self.sent.append(copy)

        def wait_in(self, slot):
            pltpu.make_async_remote_copy(
                src_ref=self.at(slot), dst_ref=self.at(slot),
                send_sem=send_sems.at[self.n, 0],
                recv_sem=recv_sems.at[self.n, slot],
                device_id=partner, device_id_type=MESH).wait_recv()

        def begin(self):
            for j in (1, 3, 2):
                self.send(self.me, self.near(j)[0])
            for j in (1, 3, 2):
                self.send(self.me, self.far(j)[0])

        def forward(self, i):
            slot = self.near(i)[1]
            self.wait_in(slot)
            for j in (1, 3, 2):
                self.send(slot, self.far(j)[0])

        def finish(self):
            for i in (0, 1, 3, 2):
                for j in (1, 3, 2):
                    self.wait_in(self.arrive(i, j))

        def drain(self):
            for copy in self.sent:
                copy.wait_send()

    def to_partner(n, src, dst):
        return pltpu.make_async_remote_copy(
            src_ref=src, dst_ref=dst, send_sem=pair_send.at[n], recv_sem=pair_recv.at[n],
            device_id=partner, device_id_type=MESH)

    def a1_at(k):
        return a1.at[:, pl.ds(pl.multiple_of(k * toks, toks), toks)]

    def b1_at(k):
        return b1.at[pl.ds(pl.multiple_of(k * toks, toks), toks), :]

    a1[:, pl.ds(pl.multiple_of(col * toks, toks), toks)] = acts[...].T
    b1[pl.ds(pl.multiple_of(row * toks, toks), toks), :] = cot[...]
    ga = Gather(0, col_axis(), a1_at)
    gb = Gather(1, row_axis(), b1_at)
    gb.begin()
    ga.begin()
    for i in (1, 3, 2):
        ga.forward(i)
        gb.forward(i)
    ga.finish()
    gb.finish()
    part[...] = jnp.dot(a1[...], b1[...], preferred_element_type=F32)
    swap = to_partner(0, part, part_in)
    swap.start()
    ga.drain()
    gb.drain()
    swap.wait()
    grad = ((part[...] + part_in[...]) * (1.0 / 64.0)).astype(BF16)

    gt_out[...] = grad.T
    remote = pltpu.make_async_remote_copy(
        src_ref=gt_out, dst_ref=gt_in, send_sem=swap_sems.at[0], recv_sem=swap_sems.at[1],
        device_id=mirror, device_id_type=MESH)
    local = pltpu.make_async_copy(gt_out, gt_in, swap_sems.at[2])

    @pl.when(off)
    def _():
        remote.start()

    @pl.when(jnp.logical_not(off))
    def _():
        local.start()

    lines = lax.broadcasted_iota(jnp.int32, (tile, tile), 0)
    places = lax.broadcasted_iota(jnp.int32, (tile, tile), 1)
    on_diag = jnp.where(off, 0.0, 1.0).astype(F32)
    identity = jnp.where(lines == places, on_diag, 0.0)
    wide = grad.astype(F32)
    trace = jnp.sum(wide * wide * (1.0 / D) + 0.9 * (stats[0] * identity))
    devs = (dev_x, dev_zl, dev_zh, dev_y)
    spots = (x, zl, zh, y)

    def trace_send(d):
        copies = []
        for j in (1, 2, 3):
            copy = pltpu.make_async_remote_copy(
                src_ref=tr.at[d, spots[d]], dst_ref=tr.at[d, spots[d]],
                send_sem=tr_send.at[d, j], recv_sem=tr_recv.at[d, spots[d]],
                device_id=devs[d](j), device_id_type=MESH)
            copy.start()
            copies.append(copy)
        return copies

    def trace_wait(d, copies):
        for j in (1, 2, 3):
            spot = (spots[d] + j) % 4
            pltpu.make_async_remote_copy(
                src_ref=tr.at[d, spot], dst_ref=tr.at[d, spot],
                send_sem=tr_send.at[d, j], recv_sem=tr_recv.at[d, spot],
                device_id=devs[d](j), device_id_type=MESH).wait_recv()
        for copy in copies:
            copy.wait_send()
        return (tr[d, 0] + tr[d, 1]) + (tr[d, 2] + tr[d, 3])

    tr[0, spots[0]] = jnp.full((8, 128), trace, F32)
    copies = trace_send(0)

    @pl.when(off)
    def _():
        remote.wait()

    @pl.when(jnp.logical_not(off))
    def _():
        local.wait()

    @pl.when(g == 0)
    def _():
        a2[col] = grad
        b2[row] = gt_in[...]

    @pl.when(g == 1)
    def _():
        a2[col] = gt_in[...]
        b2[row] = grad

    ga = Gather(2, col_axis(), lambda k: a2.at[k])
    gb = Gather(3, row_axis(), lambda k: b2.at[k])
    gb.begin()
    ga.begin()
    for d, i in ((1, 1), (2, 3), (3, 2)):
        tr[d, spots[d]] = trace_wait(d - 1, copies)
        copies = trace_send(d)
        ga.forward(i)
        gb.forward(i)
    total = trace_wait(3, copies)
    ga.finish()
    gb.finish()

    def product(left, right):
        part[...] = jnp.zeros_like(part)

        def step(k, carry):
            part[...] += jnp.dot(left[k], right[k], preferred_element_type=F32)
            return carry

        lax.fori_loop(0, 16, step, 0)

    product(a2, b2)
    stat = 0.9 * stats[0] + part[...] * (1.0 / D)
    new_stats[0] = stat
    scale = total[0:1, 0:1] * (1.0 / D)
    root = (jnp.sqrt(lax.rsqrt(scale)) * (5.0 * identity - stat / scale) * 0.25).astype(BF16)
    roots[0] = root
    gt_out[...] = root
    slot_in = (1 - g) * row + g * col
    slot_out = (1 - g) * col + g * row
    swap = to_partner(1, gt_out, p3.at[slot_out])
    swap.start()
    ga.drain()
    gb.drain()
    swap.wait_send()
    to_partner(1, gt_out, p3.at[slot_in]).wait_recv()

    @pl.when(g == 1)
    def _():
        gather = Gather(4, col_axis(), lambda k: p3.at[k])
        gather.begin()
        for i in (1, 3, 2):
            gather.forward(i)
        gather.finish()
        product(p3, b2)
        gt_out[...] = part[...].astype(BF16)
        side = to_partner(2, gt_out, p4.at[col])
        side.start()
        gather.drain()
        side.wait_send()
        to_partner(3, up_in, up_in).wait_recv()
        update[...] = up_in[...]

    @pl.when(g == 0)
    def _():
        gather = Gather(4, row_axis(), lambda k: p3.at[k])
        gather.begin()
        for i in (1, 3, 2):
            gather.forward(i)
        gather.finish()
        gather.drain()
        to_partner(2, gt_out, p4.at[col]).wait_recv()
        gather = Gather(5, col_axis(), lambda k: p4.at[k])
        gather.begin()
        for i in (1, 3, 2):
            gather.forward(i)
        gather.finish()
        product(p4, p3)
        result = part[...].astype(BF16)
        update[...] = result
        gt_out[...] = result
        final = to_partner(3, gt_out, up_in)
        final.start()
        gather.drain()
        final.wait_send()


def shards(activations, cotangent, statistics):
    toks, tile = activations.shape
    vmem = pl.BlockSpec(memory_space=pltpu.VMEM)
    return pl.pallas_call(
        kernel,
        out_shape=(
            jax.ShapeDtypeStruct((1, tile, tile), F32),
            jax.ShapeDtypeStruct((1, tile, tile), BF16),
            jax.ShapeDtypeStruct((tile, tile), BF16),
        ),
        in_specs=[vmem] * 3,
        out_specs=(vmem,) * 3,
        scratch_shapes=[
            pltpu.VMEM((tile, 16 * toks), BF16),
            pltpu.VMEM((16 * toks, tile), BF16),
            pltpu.VMEM((16, tile, tile), BF16),
            pltpu.VMEM((16, tile, tile), BF16),
            pltpu.VMEM((16, tile, tile), BF16),
            pltpu.VMEM((16, tile, tile), BF16),
            pltpu.VMEM((tile, tile), F32),
            pltpu.VMEM((tile, tile), F32),
            pltpu.VMEM((tile, tile), BF16),
            pltpu.VMEM((tile, tile), BF16),
            pltpu.VMEM((4, 4, 8, 128), F32),
            pltpu.VMEM((tile, tile), BF16),
            pltpu.SemaphoreType.DMA((6, 15)),
            pltpu.SemaphoreType.DMA((6, 16)),
            pltpu.SemaphoreType.DMA((4, 4)),
            pltpu.SemaphoreType.DMA((4, 4)),
            pltpu.SemaphoreType.DMA((4,)),
            pltpu.SemaphoreType.DMA((4,)),
            pltpu.SemaphoreType.DMA((3,)),
        ],
        compiler_params=pltpu.CompilerParams(
            collective_id=0, has_side_effects=True, vmem_limit_bytes=48 * 2**20
        ),
        cost_estimate=pl.CostEstimate(flops=3 * 10**9, bytes_accessed=2 * 10**6, transcendentals=0),
    )(activations, cotangent, statistics)


def solution(mesh):
    placed = (P(("group", "col"), "row"), P(("group", "row"), "col"), P("group", "row", "col"))
    return jax.shard_map(
        shards,
        mesh=mesh,
        in_specs=placed,
        out_specs=(P("group", "row", "col"), P("group", "row", "col"), P("row", "col")),
        check_vma=False,
    )
```

```python
import itertools

import jax
import jax.numpy as jnp
from jax import lax
from jax.experimental import pallas as pl
from jax.experimental.pallas import tpu as pltpu
from jax.sharding import PartitionSpec as P

D = 5120
MESH = pl.DeviceIdType.MESH
F32 = jnp.float32
BF16 = jnp.bfloat16
CUT = 99
MAIN, TAIL = 256, 64
PART = 80
SPLIT = (0, 208, 400)


def pack(value, dst):
    tile = value.shape[0]
    dst[0:tile, :] = value[:, :MAIN]
    for i in range(tile // PART):
        rest = value[PART * i : PART * (i + 1), MAIN:]
        dst[tile : tile + PART, TAIL * i : TAIL * (i + 1)] = rest


def unpack(src, dst):
    tile = dst.shape[0]
    dst[:, :MAIN] = src[0:tile, :]
    for i in range(tile // PART):
        rest = src[tile : tile + PART, TAIL * i : TAIL * (i + 1)]
        dst[PART * i : PART * (i + 1), MAIN:] = rest


def kernel(
    acts, cot, stats, new_stats, roots, update,
    a1, b1, gp, panel, pbuf, rsx, zbuf, rsz, rp, sp, part, part_in, own, tmp, up_in, gsum, tr,
    send_sems, recv_sems, rs_send, rs_recv, tr_send, tr_recv, pair_send, pair_recv,
):
    g = lax.axis_index("group")
    row = lax.axis_index("row")
    col = lax.axis_index("col")
    zh, y = row // 4, row % 4
    x, zl = col // 4, col % 4
    tile = stats.shape[1]
    toks = acts.shape[0]

    def sel(first, second):
        return (1 - g) * first + g * second

    def at_zl(v):
        return row, 4 * x + v

    def at_x(v):
        return row, 4 * v + zl

    def at_zh(v):
        return 4 * v + y, col

    def at_y(v):
        return 4 * zh + v, col

    def device(place):
        return (g, place[0], place[1])

    def both(first, second):
        def place(v):
            (r0, c0), (r1, c1) = first(v), second(v)
            return sel(r0, r1), sel(c0, c1)

        return place

    partner = (1 - g, row, col)
    col_axis = (zl, at_zl, x, at_x)
    row_axis = (zh, at_zh, y, at_y)
    row_col = (sel(zh, zl), both(at_zh, at_zl), sel(y, x), both(at_y, at_x))
    col_row = (sel(zl, zh), both(at_zl, at_zh), sel(x, y), both(at_x, at_y))

    barrier = pltpu.get_barrier_semaphore()
    for place, v in ((at_zl, zl), (at_x, x), (at_zh, zh), (at_y, y)):
        for j in (1, 2, 3):
            pl.semaphore_signal(
                barrier, inc=1, device_id=device(place((v + j) % 4)), device_id_type=MESH)
    pl.semaphore_signal(barrier, inc=1, device_id=partner, device_id_type=MESH)
    pl.semaphore_wait(barrier, 13)
    if CUT == 0:
        return

    def remote(src, dst, send, recv, dev):
        return pltpu.make_async_remote_copy(
            src_ref=src, dst_ref=dst, send_sem=send, recv_sem=recv,
            device_id=dev, device_id_type=MESH)

    class Gather:
        def __init__(self, index, axis, at, on_tile=None):
            self.index, self.at, self.sent = index, at, []
            self.n, self.near, self.f, self.far = axis
            self.on_tile = on_tile or (lambda nn, ff: None)

        def place(self, a, b):
            return (self.n + a) % 4, (self.f + b) % 4

        def copy(self, a, b, h, dev, sem):
            nn, ff = self.place(a, b)
            ref = self.at(nn, ff, h)
            return remote(ref, ref, send_sems.at[self.index, sem],
                          recv_sems.at[self.index, (4 * nn + ff) * 2 + h], dev)

        def send(self, a, b, h, dev):
            copy = self.copy(a, b, h, dev, len(self.sent))
            copy.start()
            self.sent.append(copy)

        def near_send(self, a, h, step):
            self.send(a, 0, h, device(self.near((self.n + step) % 4)))

        def far_send(self, a, b, h, step):
            self.send(a, b, h, device(self.far((self.f + step) % 4)))

        def wait(self, a, b, h):
            self.copy(a, b, h, partner, 0).wait_recv()

        def spread(self, a, h):
            self.far_send(a, 0, h, 1)
            self.far_send(a, 0, h, 3)

        def tile(self, a, b):
            self.on_tile(*self.place(a, b))

        def pass_on(self, a):
            self.wait(a, 3, 0)
            self.far_send(a, 3, 0, 1)
            self.wait(a, 1, 1)
            self.far_send(a, 1, 1, 3)

        def beside(self, a):
            self.wait(a, 3, 1)
            self.tile(a, 3)
            self.wait(a, 1, 0)
            self.tile(a, 1)

        def across(self, a):
            self.wait(a, 2, 0)
            self.wait(a, 2, 1)
            self.tile(a, 2)

        def steps(self):
            for h, step in ((0, 1), (1, 3), (1, 1), (0, 3)):
                self.near_send(0, h, step)
            for h, step in ((0, 1), (1, 3), (1, 1), (0, 3)):
                self.far_send(0, 0, h, step)
            self.tile(0, 0)
            yield
            self.wait(3, 0, 0)
            self.near_send(3, 0, 1)
            self.spread(3, 0)
            yield
            self.wait(1, 0, 1)
            self.near_send(1, 1, 3)
            self.spread(1, 1)
            yield
            self.pass_on(0)
            yield
            self.wait(3, 0, 1)
            self.spread(3, 1)
            self.tile(3, 0)
            yield
            self.wait(1, 0, 0)
            self.spread(1, 0)
            self.tile(1, 0)
            yield
            self.beside(0)
            yield
            self.wait(2, 0, 0)
            self.spread(2, 0)
            self.pass_on(3)
            yield
            self.wait(2, 0, 1)
            self.spread(2, 1)
            self.tile(2, 0)
            self.pass_on(1)
            yield
            self.across(0)
            self.beside(3)
            yield
            self.beside(1)
            yield
            self.pass_on(2)
            yield
            self.across(3)
            self.across(1)
            yield
            self.beside(2)
            self.across(2)

        def run(self):
            for _ in self.steps():
                pass

        def drain(self):
            for copy in self.sent:
                copy.wait_send()

    def to_partner(n, src, dst):
        return remote(src, dst, pair_send.at[n], pair_recv.at[n], partner)

    def packed(buffer):
        def at(nn, ff, h):
            return buffer.at[4 * nn + ff, pl.ds(SPLIT[h], SPLIT[h + 1] - SPLIT[h]), :]

        return at

    def strip(buffer, order):
        def at(nn, ff, h):
            lanes = pl.ds(pl.multiple_of(order(nn, ff) * toks, toks), toks)
            return buffer.at[pl.ds(h * (tile // 2), tile // 2), lanes]

        return at

    a1[:, pl.ds(pl.multiple_of(col * toks, toks), toks)] = acts[...].T
    b1[:, pl.ds(pl.multiple_of(row * toks, toks), toks)] = cot[...].T
    ga = Gather(0, col_axis, strip(a1, lambda nn, ff: 4 * ff + nn))
    gb = Gather(1, row_axis, strip(b1, lambda nn, ff: 4 * nn + ff))
    for _ in itertools.zip_longest(gb.steps(), ga.steps()):
        pass
    for gather in (ga, gb):
        gather.drain()
    if CUT == 1:
        return
    part[...] = lax.dot_general(
        a1[...], b1[...], (((1,), (1,)), ((), ())), preferred_element_type=F32)
    swap = to_partner(0, part, part_in)
    swap.start()
    swap.wait()
    grad = ((part[...] + part_in[...]) * (1.0 / 64.0)).astype(BF16)
    if CUT == 2:
        update[...] = grad
        return

    lines = lax.broadcasted_iota(jnp.int32, (tile, tile), 0)
    places = lax.broadcasted_iota(jnp.int32, (tile, tile), 1)
    identity = jnp.where((lines == places) & (row == col), 1.0, 0.0).astype(F32)
    spots = ((x, at_x), (zl, at_zl), (zh, at_zh), (y, at_y))

    def trace_copy(d, j, spot):
        v, place = spots[d]
        return remote(tr.at[d, spot], tr.at[d, spot], tr_send.at[d, j], tr_recv.at[d, spot],
                      device(place((v + j) % 4)))

    def trace_send(d, value):
        v = spots[d][0]
        tr[d, v] = value
        for j in (1, 2, 3):
            trace_copy(d, j, v).start()

    def trace_wait(d):
        v = spots[d][0]
        for j in (1, 2, 3):
            trace_copy(d, j, (v + j) % 4).wait_recv()
        for j in (1, 2, 3):
            trace_copy(d, j, v).wait_send()
        return (tr[d, 0] + tr[d, 1]) + (tr[d, 2] + tr[d, 3])

    own[...] = grad
    n, f = row_col[0], row_col[2]
    fast, at_fast = sel(x, y), both(at_x, at_y)
    slow, at_slow = sel(zl, zh), both(at_zl, at_zh)

    @pl.when(g == 0)
    def _():
        pack(grad, gp.at[4 * n + f])

    @pl.when(g == 1)
    def _():
        pack(grad.T, gp.at[4 * n + f])

    def fast_copy(nn, ff):
        return remote(pbuf.at[4 * nn + ff], rsx.at[4 * ff + fast],
                      rs_send.at[4 * nn + ff], rs_recv.at[4 * ff + fast], device(at_fast(nn)))

    def slow_copy(ff):
        return remote(zbuf.at[ff], rsz.at[slow], rs_send.at[16 + ff], rs_recv.at[16 + slow],
                      device(at_slow(ff)))

    def gram_term(nn, ff):
        slot = 4 * nn + ff
        unpack(gp.at[slot], panel.at[slot])

        @pl.when(g == 0)
        def _():
            term = lax.dot_general(
                own[...], panel[slot], (((1,), (1,)), ((), ())), preferred_element_type=F32)
            pack(term.astype(BF16), pbuf.at[slot])

        @pl.when(g == 1)
        def _():
            term = jnp.dot(panel[slot], own[...], preferred_element_type=F32)
            pack(term.astype(BF16), pbuf.at[slot])

        @pl.when(nn != fast)
        def _():
            fast_copy(nn, ff).start()

    def reduce_fast(b):
        ff = (f + b) % 4
        total = pbuf[4 * fast + ff].astype(F32)
        for e in (1, 3, 2):
            other = 4 * ff + (fast + e) % 4
            remote(pbuf.at[0], rsx.at[other], rs_send.at[0], rs_recv.at[other],
                   partner).wait_recv()
            total = total + rsx[other].astype(F32)
        zbuf[ff] = total.astype(BF16)

        @pl.when(ff != slow)
        def _():
            slow_copy(ff).start()

    gather = Gather(2, row_col, packed(gp), gram_term)
    sums = {}

    def trace_step(d):
        trace_send(d, trace_wait(d - 1))

    for k, _ in enumerate(gather.steps()):
        if k == 0:
            wide = grad.astype(F32)
            trace = jnp.sum(wide * wide * (1.0 / D) + 0.9 * (stats[0] * identity))
            trace_send(0, jnp.full((8, 128), trace, F32))
        if k in (2, 4, 6):
            trace_step(k // 2)
        if k == 8:
            total_trace = trace_wait(3)
        if k == 9:
            reduce_fast(0)
        if CUT == 3 and k == 2:
            pass
    for b in (1, 3, 2):
        reduce_fast(b)
    gram = zbuf[slow].astype(F32)
    for e in (1, 3, 2):
        other = (slow + e) % 4
        remote(zbuf.at[0], rsz.at[other], rs_send.at[16], rs_recv.at[16 + other],
               partner).wait_recv()
        gram = gram + rsz[other].astype(F32)
    gsum[...] = gram
    unpack(gsum, part)
    gather.drain()
    for a in range(4):
        for b in range(4):
            nn, ff = gather.place(a, b)

            @pl.when(nn != fast)
            def _():
                fast_copy(nn, ff).wait_send()

    for b in range(4):
        ff = (f + b) % 4

        @pl.when(ff != slow)
        def _():
            slow_copy(ff).wait_send()

    if CUT == 4:
        return
    stat = 0.9 * stats[0] + part[...] * (1.0 / D)
    new_stats[0] = stat
    scale = total_trace[0:1, 0:1] * (1.0 / D)
    root = (jnp.sqrt(lax.rsqrt(scale)) * (5.0 * identity - stat / scale) * 0.25).astype(BF16)
    roots[0] = root
    n, f = col_row[0], col_row[2]
    pack(root, rp.at[4 * n + f])
    if CUT == 5:
        return

    @pl.when(g == 0)
    def _():
        part[...] = jnp.zeros_like(part)

        def side_term(nn, ff):
            unpack(rp.at[4 * nn + ff], tmp)
            part[...] += jnp.dot(tmp[...], panel[4 * ff + nn], preferred_element_type=F32)

        gather = Gather(3, col_row, packed(rp), side_term)
        gather.run()
        if CUT == 6:
            gather.drain()
            return
        pack(part[...].astype(BF16), gp.at[0])
        side = to_partner(1, gp.at[0], sp.at[4 * zl + x])
        side.start()
        gather.drain()
        side.wait_send()
        to_partner(2, up_in, up_in).wait_recv()
        update[...] = up_in[...]

    @pl.when(g == 1)
    def _():
        def keep(nn, ff):
            unpack(rp.at[4 * nn + ff], panel.at[4 * nn + ff])

        gather = Gather(3, col_row, packed(rp), keep)
        gather.run()
        gather.drain()
        if CUT == 6:
            return
        part[...] = jnp.zeros_like(part)
        to_partner(1, gp.at[0], sp.at[4 * zl + x]).wait_recv()

        def update_term(nn, ff):
            unpack(sp.at[4 * nn + ff], tmp)
            part[...] += jnp.dot(tmp[...], panel[4 * ff + nn], preferred_element_type=F32)

        gather = Gather(4, col_axis, packed(sp), update_term)
        gather.run()
        result = part[...].astype(BF16)
        update[...] = result
        own[...] = result
        final = to_partner(2, own, up_in)
        final.start()
        gather.drain()
        final.wait_send()


def shards(activations, cotangent, statistics):
    toks, tile = activations.shape
    vmem = pl.BlockSpec(memory_space=pltpu.VMEM)
    compact = (tile + PART, MAIN)
    return pl.pallas_call(
        kernel,
        out_shape=(
            jax.ShapeDtypeStruct((1, tile, tile), F32),
            jax.ShapeDtypeStruct((1, tile, tile), BF16),
            jax.ShapeDtypeStruct((tile, tile), BF16),
        ),
        in_specs=[vmem] * 3,
        out_specs=(vmem,) * 3,
        scratch_shapes=[
            pltpu.VMEM((tile, 16 * toks), BF16),
            pltpu.VMEM((tile, 16 * toks), BF16),
            pltpu.VMEM((16,) + compact, BF16),
            pltpu.VMEM((16, tile, tile), BF16),
            pltpu.VMEM((16,) + compact, BF16),
            pltpu.VMEM((16,) + compact, BF16),
            pltpu.VMEM((4,) + compact, BF16),
            pltpu.VMEM((4,) + compact, BF16),
            pltpu.VMEM((16,) + compact, BF16),
            pltpu.VMEM((16,) + compact, BF16),
            pltpu.VMEM((tile, tile), F32),
            pltpu.VMEM((tile, tile), F32),
            pltpu.VMEM((tile, tile), BF16),
            pltpu.VMEM((tile, tile), BF16),
            pltpu.VMEM((tile, tile), BF16),
            pltpu.VMEM(compact, F32),
            pltpu.VMEM((4, 4, 8, 128), F32),
            pltpu.SemaphoreType.DMA((5, 30)),
            pltpu.SemaphoreType.DMA((5, 32)),
            pltpu.SemaphoreType.DMA((20,)),
            pltpu.SemaphoreType.DMA((20,)),
            pltpu.SemaphoreType.DMA((4, 4)),
            pltpu.SemaphoreType.DMA((4, 4)),
            pltpu.SemaphoreType.DMA((3,)),
            pltpu.SemaphoreType.DMA((3,)),
        ],
        compiler_params=pltpu.CompilerParams(
            collective_id=0, has_side_effects=True, vmem_limit_bytes=48 * 2**20
        ),
        cost_estimate=pl.CostEstimate(flops=3 * 10**9, bytes_accessed=2 * 10**6, transcendentals=0),
    )(activations, cotangent, statistics)


def solution(mesh):
    placed = (P(("group", "col"), "row"), P(("group", "row"), "col"), P("group", "row", "col"))
    return jax.shard_map(
        shards,
        mesh=mesh,
        in_specs=placed,
        out_specs=(P("group", "row", "col"), P("group", "row", "col"), P("row", "col")),
        check_vma=False,
    )
```

```python
import itertools

import jax
import jax.numpy as jnp
from jax import lax
from jax.experimental import pallas as pl
from jax.experimental.pallas import tpu as pltpu
from jax.sharding import PartitionSpec as P

D = 5120
MESH = pl.DeviceIdType.MESH
F32 = jnp.float32
BF16 = jnp.bfloat16
CUT = 99
MAIN, TAIL = 256, 64
RESTS = ((0, 48), (48, 96), (96, 144), (144, 160))
HALF = 160
PACKED = HALF + 48


def pack(value, dst):
    dst[0:HALF, :] = value[:, :MAIN]
    for i, (lo, hi) in enumerate(RESTS):
        dst[HALF : HALF + hi - lo, TAIL * i : TAIL * (i + 1)] = value[lo:hi, MAIN:]


def unpack(src, dst):
    dst[:, :MAIN] = src[0:HALF, :]
    for i, (lo, hi) in enumerate(RESTS):
        dst[lo:hi, MAIN:] = src[HALF : HALF + hi - lo, TAIL * i : TAIL * (i + 1)]


def kernel(
    acts, cot, stats, new_stats, roots, update,
    a1, b1, own, ownt, zt, bq, bp, gb, ax, au, tq, tu, t_out, lz_out, lz_in, rx_out, rx_in,
    swap_out, swap_in, part, part_in, gsum, lt, sx_out, sx_in, rp, sp, panel, tmp, up_in, tr,
    send_sems, recv_sems, ss, rs, tr_send, tr_recv,
):
    g = lax.axis_index("group")
    row = lax.axis_index("row")
    col = lax.axis_index("col")
    zh, y = row // 4, row % 4
    x, zl = col // 4, col % 4
    tile = stats.shape[1]
    toks = acts.shape[0]

    def sel(first, second):
        return (1 - g) * first + g * second

    def at_zl(v):
        return row, 4 * x + v

    def at_x(v):
        return row, 4 * v + zl

    def at_zh(v):
        return 4 * v + y, col

    def at_y(v):
        return 4 * zh + v, col

    def device(place):
        return (g, place[0], place[1])

    def both(first, second):
        def place(v):
            (r0, c0), (r1, c1) = first(v), second(v)
            return sel(r0, r1), sel(c0, c1)

        return place

    partner = (1 - g, row, col)
    mirror = (g, col, row)
    off = row != col
    col_axis = (zl, at_zl, x, at_x)
    row_axis = (zh, at_zh, y, at_y)

    barrier = pltpu.get_barrier_semaphore()
    for place, v in ((at_zl, zl), (at_x, x), (at_zh, zh), (at_y, y)):
        for j in (1, 2, 3):
            pl.semaphore_signal(
                barrier, inc=1, device_id=device(place((v + j) % 4)), device_id_type=MESH)
    pl.semaphore_signal(barrier, inc=1, device_id=partner, device_id_type=MESH)

    @pl.when(off)
    def _():
        pl.semaphore_signal(barrier, inc=1, device_id=mirror, device_id_type=MESH)
        pl.semaphore_wait(barrier, 14)

    @pl.when(jnp.logical_not(off))
    def _():
        pl.semaphore_wait(barrier, 13)

    if CUT == 0:
        return

    def remote(src, dst, send, recv, dev):
        return pltpu.make_async_remote_copy(
            src_ref=src, dst_ref=dst, send_sem=send, recv_sem=recv,
            device_id=dev, device_id_type=MESH)

    class Gather:
        def __init__(self, index, axis, at, on_tile=None):
            self.index, self.at, self.sent = index, at, []
            self.n, self.near, self.f, self.far = axis
            self.on_tile = on_tile or (lambda nn, ff: None)

        def place(self, a, b):
            return (self.n + a) % 4, (self.f + b) % 4

        def copy(self, a, b, h, dev, sem):
            nn, ff = self.place(a, b)
            ref = self.at(nn, ff, h)
            return remote(ref, ref, send_sems.at[self.index, sem],
                          recv_sems.at[self.index, (4 * nn + ff) * 2 + h], dev)

        def send(self, a, b, h, dev):
            copy = self.copy(a, b, h, dev, len(self.sent))
            copy.start()
            self.sent.append(copy)

        def near_send(self, a, h, step):
            self.send(a, 0, h, device(self.near((self.n + step) % 4)))

        def far_send(self, a, b, h, step):
            self.send(a, b, h, device(self.far((self.f + step) % 4)))

        def wait(self, a, b, h):
            self.copy(a, b, h, partner, 0).wait_recv()

        def spread(self, a, h):
            self.far_send(a, 0, h, 1)
            self.far_send(a, 0, h, 3)

        def tile(self, a, b):
            self.on_tile(*self.place(a, b))

        def pass_on(self, a):
            self.wait(a, 3, 0)
            self.far_send(a, 3, 0, 1)
            self.wait(a, 1, 1)
            self.far_send(a, 1, 1, 3)

        def beside(self, a):
            self.wait(a, 3, 1)
            self.tile(a, 3)
            self.wait(a, 1, 0)
            self.tile(a, 1)

        def across(self, a):
            self.wait(a, 2, 0)
            self.wait(a, 2, 1)
            self.tile(a, 2)

        def steps(self):
            for h, step in ((0, 1), (1, 3), (1, 1), (0, 3)):
                self.near_send(0, h, step)
            for h, step in ((0, 1), (1, 3), (1, 1), (0, 3)):
                self.far_send(0, 0, h, step)
            self.tile(0, 0)
            yield
            self.wait(3, 0, 0)
            self.near_send(3, 0, 1)
            self.spread(3, 0)
            yield
            self.wait(1, 0, 1)
            self.near_send(1, 1, 3)
            self.spread(1, 1)
            yield
            self.pass_on(0)
            yield
            self.wait(3, 0, 1)
            self.spread(3, 1)
            self.tile(3, 0)
            yield
            self.wait(1, 0, 0)
            self.spread(1, 0)
            self.tile(1, 0)
            yield
            self.beside(0)
            yield
            self.wait(2, 0, 0)
            self.spread(2, 0)
            self.pass_on(3)
            yield
            self.wait(2, 0, 1)
            self.spread(2, 1)
            self.tile(2, 0)
            self.pass_on(1)
            yield
            self.across(0)
            self.beside(3)
            yield
            self.beside(1)
            yield
            self.pass_on(2)
            yield
            self.across(3)
            self.across(1)
            yield
            self.beside(2)
            self.across(2)

        def run(self):
            for _ in self.steps():
                pass

        def drain(self):
            for copy in self.sent:
                copy.wait_send()

    used = [0]

    def take(count):
        used[0] += count
        return used[0] - count

    class Fan:
        def __init__(self, v, place, out, into):
            self.v, self.place, self.out, self.into = v, place, out, into
            self.base = take(4)

        def copy(self, to):
            return remote(self.out(to), self.into(self.v), ss.at[self.base + to],
                          rs.at[self.base + self.v], device(self.place(to)))

        def send(self, e):
            self.copy((self.v + e) % 4).start()

        def send_to(self, to):
            @pl.when(to != self.v)
            def _():
                self.copy(to).start()

        def wait(self, e):
            source = (self.v + e) % 4
            remote(self.out(self.v), self.into(source), ss.at[self.base],
                   rs.at[self.base + source], partner).wait_recv()

        def drain(self):
            for e in (1, 2, 3):
                self.copy((self.v + e) % 4).wait_send()

        def total(self):
            value = self.out(self.v)[...].astype(F32)
            for e in (1, 3, 2):
                self.wait(e)
                value = value + self.into((self.v + e) % 4)[...].astype(F32)
            return value

    def gather_fan(v, place, buffer):
        return Fan(v, place, lambda to: buffer.at[v], lambda source: buffer.at[source])

    def sum_fan(v, place, out, into):
        return Fan(v, place, lambda to: out.at[to], lambda source: into.at[source])

    pair_base = take(8)

    def to_partner(n, src, dst):
        return remote(src, dst, ss.at[pair_base + n], rs.at[pair_base + n], partner)

    def packed(buffer):
        def at(nn, ff, h):
            return buffer.at[4 * nn + ff, pl.ds(PACKED * h, PACKED), :]

        return at

    def strip(buffer, order):
        def at(nn, ff, h):
            lanes = pl.ds(pl.multiple_of(order(nn, ff) * toks, toks), toks)
            return buffer.at[pl.ds(h * (tile // 2), tile // 2), lanes]

        return at

    a1[:, pl.ds(pl.multiple_of(col * toks, toks), toks)] = acts[...].T
    b1[:, pl.ds(pl.multiple_of(row * toks, toks), toks)] = cot[...].T
    ga = Gather(0, col_axis, strip(a1, lambda nn, ff: 4 * ff + nn))
    gc = Gather(1, row_axis, strip(b1, lambda nn, ff: 4 * nn + ff))
    for _ in itertools.zip_longest(gc.steps(), ga.steps()):
        pass
    for gather in (ga, gc):
        gather.drain()
    if CUT == 1:
        return
    part[...] = lax.dot_general(
        a1[...], b1[...], (((1,), (1,)), ((), ())), preferred_element_type=F32)
    swap = to_partner(0, part, part_in)
    swap.start()
    swap.wait()
    grad = ((part[...] + part_in[...]) * (1.0 / 64.0)).astype(BF16)
    if CUT == 2:
        update[...] = grad
        return

    lines = lax.broadcasted_iota(jnp.int32, (tile, tile), 0)
    places = lax.broadcasted_iota(jnp.int32, (tile, tile), 1)
    identity = jnp.where((lines == places) & (row == col), 1.0, 0.0).astype(F32)
    spots = ((x, at_x), (zl, at_zl), (zh, at_zh), (y, at_y))

    def trace_copy(d, j, spot):
        v, place = spots[d]
        return remote(tr.at[d, spot], tr.at[d, spot], tr_send.at[d, j], tr_recv.at[d, spot],
                      device(place((v + j) % 4)))

    def trace_send(d, value):
        v = spots[d][0]
        tr[d, v] = value
        for j in (1, 2, 3):
            trace_copy(d, j, v).start()

    def trace_wait(d):
        v = spots[d][0]
        for j in (1, 2, 3):
            trace_copy(d, j, (v + j) % 4).wait_recv()
        for j in (1, 2, 3):
            trace_copy(d, j, v).wait_send()
        return (tr[d, 0] + tr[d, 1]) + (tr[d, 2] + tr[d, 3])

    fwd, back = 1 + 2 * g, 3 - 2 * g
    mine = pl.ds(pl.multiple_of(HALF * g, HALF), HALF)
    other = pl.ds(pl.multiple_of(HALF * (1 - g), HALF), HALF)
    own[...] = grad
    ownt[...] = grad.T
    pack(own[mine, :], zt.at[zh])
    ax[x] = zt[zh]
    pack(ownt[mine, :], t_out)

    zs, zr = take(4), take(4)

    def ring_copy(index, step, sem):
        return remote(zt.at[index], zt.at[index], ss.at[zs + sem], rs.at[zr + index],
                      device(at_zh((zh + step) % 4)))

    across = Fan(x, at_x, lambda to: zt.at[to], lambda source: bq.at[4 * y + source])

    def turn(a):
        index = (zh + a) % 4
        across.send_to(index)

        @pl.when(index == x)
        def _():
            bq[4 * y + x] = zt[x]

    def ring_wait(a):
        ring_copy((zh + a) % 4, 1, 0).wait_recv()

    ys, yr, ps = take(16), take(16), take(16)

    def y_copy(b, e, step, sem):
        slot = 4 * ((y + b) % 4) + (x + e) % 4
        return remote(bq.at[slot], bq.at[slot], ss.at[ys + 4 * e + sem], rs.at[yr + slot],
                      device(at_y((y + step) % 4)))

    def hand_over(b):
        place = (y + b) % 4
        four = pl.ds(4 * place, 4)
        return remote(bq.at[four], bp.at[four], ss.at[ps + place], rs.at[ps + place], partner)

    ring = (0, 1, 3, 2)
    acts_fan = gather_fan(x, at_x, ax)
    left_fan = sum_fan(zl, at_zl, lz_out, lz_in)
    right_fan = sum_fan(x, at_x, rx_out, rx_in)
    gt_fan = gather_fan(zl, at_zl, tq)

    def left_group(b):
        place = (y + b) % 4
        hand_over(b).wait_recv()
        acc = jnp.zeros((HALF, tile), F32)
        for e in range(4):
            slot = 4 * place + (x + e) % 4
            unpack(bq.at[slot], gb.at[slot, mine, :])
            unpack(bp.at[slot], gb.at[slot, other, :])
            acc += lax.dot_general(au[(x + e) % 4], gb[slot], (((1,), (1,)), ((), ())),
                                   preferred_element_type=F32)
        pack(acc.astype(BF16), lz_out.at[place])
        left_fan.send_to(place)

    def product(left, fan, out):
        for e in (1, 3, 2, 0):
            index = (x + e) % 4
            acc = jnp.zeros((HALF, tile), F32)
            for k in range(4):
                acc += jnp.dot(left[k], gb[4 * k + index], preferred_element_type=F32)
            pack(acc.astype(BF16), out.at[index])
            if e:
                fan.send(e)

    def trace_step(d):
        trace_send(d, trace_wait(d - 1))

    flip = take(1)
    flip_copy = remote(t_out, tq.at[y], ss.at[flip], rs.at[flip], mirror)

    for step in (1, 3):
        ring_copy(zh, step, step).start()
    turn(0)
    for e in (1, 3, 2):
        acts_fan.send(e)
    wide = grad.astype(F32)
    trace = jnp.sum(wide * wide * (1.0 / D) + 0.9 * (stats[0] * identity))
    trace_send(0, jnp.full((8, 128), trace, F32))
    ring_wait(back)
    ring_copy((zh + back) % 4, fwd, 2).start()
    turn(back)

    ring_wait(fwd)
    turn(fwd)
    trace_step(1)
    ring_wait(2)
    turn(2)
    @pl.when(off)
    def _():
        flip_copy.start()

    @pl.when(jnp.logical_not(off))
    def _():
        tq[zl] = t_out[...]

    for e in ring:
        if e:
            across.wait(e)
        y_copy(0, e, 1, 0).start()
        y_copy(0, e, 3, 1).start()
    hand_over(0).start()
    trace_step(2)
    for e in (1, 3, 2):
        acts_fan.wait(e)
    for k in range(4):
        unpack(ax.at[k], au.at[k])
    for e in ring:
        y_copy(back, e, 1, 0).wait_recv()
        y_copy(back, e, fwd, 2).start()
    hand_over(back).start()
    left_group(0)
    trace_step(3)

    @pl.when(off)
    def _():
        remote(t_out, tq.at[zl], ss.at[flip], rs.at[flip], mirror).wait_recv()

    for e in (1, 3, 2):
        gt_fan.send(e)
    for e in ring:
        y_copy(fwd, e, 1, 0).wait_recv()
    hand_over(fwd).start()
    left_group(back)
    for e in ring:
        y_copy(2, e, 1, 0).wait_recv()
    hand_over(2).start()
    left_group(fwd)
    left_group(2)
    total_trace = trace_wait(3)
    for e in (1, 3, 2):
        gt_fan.wait(e)
    for k in range(4):
        unpack(tq.at[k], tu.at[k])
    product(tu, right_fan, rx_out)
    left_sum = left_fan.total()
    gsum[0] = left_sum
    right_sum = right_fan.total()
    gsum[1] = right_sum
    unpack(gsum.at[g], part.at[mine, :])
    unpack(gsum.at[1 - g], swap_out)
    swap = to_partner(1, swap_out, swap_in)
    swap.start()
    for fan in (acts_fan, left_fan, right_fan, gt_fan):
        fan.drain()
    for e in (1, 2, 3):
        across.copy((x + e) % 4).wait_send()
    for sem in (1, 3, 2):
        ring_copy(zh, 1, sem).wait_send()
    for e in range(4):
        for sem in range(3):
            y_copy(0, e, 1, sem).wait_send()
        hand_over(e).wait_send()

    @pl.when(off)
    def _():
        flip_copy.wait_send()

    swap.wait()
    part[other, :] = swap_in[...]
    if CUT == 4:
        return
    stat = 0.9 * stats[0] + part[...] * (1.0 / D)
    new_stats[0] = stat
    scale = total_trace[0:1, 0:1] * (1.0 / D)
    root = (jnp.sqrt(lax.rsqrt(scale)) * (5.0 * identity - stat / scale) * 0.25).astype(BF16)
    roots[0] = root
    own[...] = root
    left_root_fan = gather_fan(zl, at_zl, lt)
    side_fan = sum_fan(x, at_x, sx_out, sx_in)

    def unpack_tile(src, dst):
        unpack(src.at[0:PACKED, :], dst.at[0:HALF, :])
        unpack(src.at[PACKED : 2 * PACKED, :], dst.at[HALF : 2 * HALF, :])

    def side_product(between):
        for e in (1, 3, 2):
            left_root_fan.wait(e)
        between()
        for k in range(4):
            unpack(lt.at[k], tu.at[k])
        product(tu, side_fan, sx_out)
        return side_fan.total().astype(BF16)

    slot = 4 * zl + x
    spot = 4 * zh + y
    rb = take(16)

    def give_right(index):
        return remote(rp.at[index], rp.at[index], ss.at[rb + index], rs.at[rb + index], partner)

    @pl.when(g == 0)
    def _():
        pack(own[HALF:, :], t_out)
        give = to_partner(2, t_out, lt.at[zl])
        give.start()
        pack(own[:HALF, :], lt.at[zl])
        for e in (1, 3, 2):
            left_root_fan.send(e)

        def keep(nn, ff):
            @pl.when(4 * nn + ff != spot)
            def _():
                give_right(4 * nn + ff).start()

        rights = Gather(2, row_axis, packed(rp), keep)
        steps = rights.steps()

        def between():
            to_partner(5, rp.at[spot], rp.at[spot]).wait_recv()
            next(steps)

        zt[0] = side_product(between)
        side = to_partner(3, zt.at[0], sp.at[slot, pl.ds(0, PACKED), :])
        side.start()
        for _ in steps:
            pass
        left_root_fan.drain()
        side_fan.drain()
        rights.drain()
        give.wait_send()
        side.wait_send()
        for k in range(1, 16):
            give_right((spot + k) % 16).wait_send()
        to_partner(4, up_in, up_in).wait_recv()
        update[...] = up_in[...]

    @pl.when(g == 1)
    def _():
        pack(own[:HALF, :], rp.at[spot, 0:PACKED, :])
        pack(own[HALF:, :], rp.at[spot, PACKED : 2 * PACKED, :])
        give = to_partner(5, rp.at[spot], rp.at[spot])
        give.start()
        to_partner(2, t_out, lt.at[zl]).wait_recv()
        for e in (1, 3, 2):
            left_root_fan.send(e)
        sp[slot, PACKED : 2 * PACKED, :] = side_product(lambda: None)
        part[...] = jnp.zeros_like(part)
        to_partner(3, zt.at[0], sp.at[slot, pl.ds(0, PACKED), :]).wait_recv()
        early, late = [], []

        def update_term(nn, ff):
            index = 4 * ff + nn

            @pl.when(index != spot)
            def _():
                give_right(index).wait_recv()

            unpack_tile(sp.at[4 * nn + ff], tmp)
            unpack_tile(rp.at[index], panel)
            part[...] += jnp.dot(tmp[...], panel[...], preferred_element_type=F32)

        def arrived(nn, ff):
            if late:
                update_term(nn, ff)
            else:
                early.append((nn, ff))

        gather = Gather(3, col_axis, packed(sp), arrived)
        for k, _ in enumerate(gather.steps()):
            if k == 8:
                late.append(k)
                for nn, ff in early:
                    update_term(nn, ff)
        result = part[...].astype(BF16)
        update[...] = result
        own[...] = result
        final = to_partner(4, own, up_in)
        final.start()
        give.wait_send()
        left_root_fan.drain()
        side_fan.drain()
        gather.drain()
        final.wait_send()


def shards(activations, cotangent, statistics):
    toks, tile = activations.shape
    vmem = pl.BlockSpec(memory_space=pltpu.VMEM)
    half = (PACKED, MAIN)
    quad, many = pltpu.VMEM((4,) + half, BF16), pltpu.VMEM((16,) + half, BF16)
    pairs = pltpu.VMEM((16, 2 * PACKED, MAIN), BF16)
    strips = pltpu.VMEM((tile, 16 * toks), BF16)
    whole = pltpu.VMEM((tile, tile), BF16)
    halves = pltpu.VMEM((4, HALF, tile), BF16)
    return pl.pallas_call(
        kernel,
        out_shape=(
            jax.ShapeDtypeStruct((1, tile, tile), F32),
            jax.ShapeDtypeStruct((1, tile, tile), BF16),
            jax.ShapeDtypeStruct((tile, tile), BF16),
        ),
        in_specs=[vmem] * 3,
        out_specs=(vmem,) * 3,
        scratch_shapes=[
            strips, strips, whole, whole, quad, many, many, pltpu.VMEM((16, tile, tile), BF16),
            quad, halves, quad, halves, pltpu.VMEM(half, BF16), quad, quad, quad, quad,
            pltpu.VMEM((HALF, tile), F32), pltpu.VMEM((HALF, tile), F32),
            pltpu.VMEM((tile, tile), F32), pltpu.VMEM((tile, tile), F32),
            pltpu.VMEM((2,) + half, F32), quad, quad, quad, pairs, pairs,
            whole, whole, whole, pltpu.VMEM((4, 4, 8, 128), F32),
            pltpu.SemaphoreType.DMA((4, 30)),
            pltpu.SemaphoreType.DMA((4, 32)),
            pltpu.SemaphoreType.DMA((112,)),
            pltpu.SemaphoreType.DMA((112,)),
            pltpu.SemaphoreType.DMA((4, 4)),
            pltpu.SemaphoreType.DMA((4, 4)),
        ],
        compiler_params=pltpu.CompilerParams(
            collective_id=0, has_side_effects=True, vmem_limit_bytes=48 * 2**20
        ),
        cost_estimate=pl.CostEstimate(flops=3 * 10**9, bytes_accessed=2 * 10**6, transcendentals=0),
    )(activations, cotangent, statistics)


def solution(mesh):
    placed = (P(("group", "col"), "row"), P(("group", "row"), "col"), P("group", "row", "col"))
    return jax.shard_map(
        shards,
        mesh=mesh,
        in_specs=placed,
        out_specs=(P("group", "row", "col"), P("group", "row", "col"), P("row", "col")),
        check_vma=False,
    )
```

```python
import itertools

import jax
import jax.numpy as jnp
from jax import lax
from jax.experimental import pallas as pl
from jax.experimental.pallas import tpu as pltpu
from jax.sharding import PartitionSpec as P

D = 5120
MESH = pl.DeviceIdType.MESH
F32 = jnp.float32
BF16 = jnp.bfloat16
CUT = 99
MAIN, TAIL = 256, 64
RESTS = ((0, 48), (48, 96), (96, 144), (144, 160))
HALF = 160
PACKED = HALF + 48


def pack(value, dst):
    dst[0:HALF, :] = value[:, :MAIN]
    for i, (lo, hi) in enumerate(RESTS):
        dst[HALF : HALF + hi - lo, TAIL * i : TAIL * (i + 1)] = value[lo:hi, MAIN:]


def unpack(src, dst):
    dst[:, :MAIN] = src[0:HALF, :]
    for i, (lo, hi) in enumerate(RESTS):
        dst[lo:hi, MAIN:] = src[HALF : HALF + hi - lo, TAIL * i : TAIL * (i + 1)]


def kernel(
    acts, cot, stats, new_stats, roots, update,
    a1, b1, own, ownt, zt, bq, bp, gb, ax, au, tq, tu, t_out, lz_out, lz_in, rx_out, rx_in,
    swap_out, swap_in, part, part_in, gsum, lt, sx_out, sx_in, rp, sp, panel, tmp, up_in, tr,
    send_sems, recv_sems, ss, rs, tr_send, tr_recv,
):
    g = lax.axis_index("group")
    row = lax.axis_index("row")
    col = lax.axis_index("col")
    zh, y = row // 4, row % 4
    x, zl = col // 4, col % 4
    tile = stats.shape[1]
    toks = acts.shape[0]

    def sel(first, second):
        return (1 - g) * first + g * second

    def at_zl(v):
        return row, 4 * x + v

    def at_x(v):
        return row, 4 * v + zl

    def at_zh(v):
        return 4 * v + y, col

    def at_y(v):
        return 4 * zh + v, col

    def device(place):
        return (g, place[0], place[1])

    def both(first, second):
        def place(v):
            (r0, c0), (r1, c1) = first(v), second(v)
            return sel(r0, r1), sel(c0, c1)

        return place

    partner = (1 - g, row, col)
    mirror = (g, col, row)
    off = row != col
    col_axis = (zl, at_zl, x, at_x)
    row_axis = (zh, at_zh, y, at_y)

    barrier = pltpu.get_barrier_semaphore()
    for place, v in ((at_zl, zl), (at_x, x), (at_zh, zh), (at_y, y)):
        for j in (1, 2, 3):
            pl.semaphore_signal(
                barrier, inc=1, device_id=device(place((v + j) % 4)), device_id_type=MESH)
    pl.semaphore_signal(barrier, inc=1, device_id=partner, device_id_type=MESH)

    @pl.when(off)
    def _():
        pl.semaphore_signal(barrier, inc=1, device_id=mirror, device_id_type=MESH)
        pl.semaphore_wait(barrier, 14)

    @pl.when(jnp.logical_not(off))
    def _():
        pl.semaphore_wait(barrier, 13)

    if CUT == 0:
        return

    def remote(src, dst, send, recv, dev):
        return pltpu.make_async_remote_copy(
            src_ref=src, dst_ref=dst, send_sem=send, recv_sem=recv,
            device_id=dev, device_id_type=MESH)

    class Gather:
        def __init__(self, index, axis, at, on_tile=None):
            self.index, self.at, self.sent = index, at, []
            self.n, self.near, self.f, self.far = axis
            self.on_tile = on_tile or (lambda nn, ff: None)

        def place(self, a, b):
            return (self.n + a) % 4, (self.f + b) % 4

        def copy(self, a, b, h, dev, sem):
            nn, ff = self.place(a, b)
            ref = self.at(nn, ff, h)
            return remote(ref, ref, send_sems.at[self.index, sem],
                          recv_sems.at[self.index, (4 * nn + ff) * 2 + h], dev)

        def send(self, a, b, h, dev):
            copy = self.copy(a, b, h, dev, len(self.sent))
            copy.start()
            self.sent.append(copy)

        def near_send(self, a, h, step):
            self.send(a, 0, h, device(self.near((self.n + step) % 4)))

        def far_send(self, a, b, h, step):
            self.send(a, b, h, device(self.far((self.f + step) % 4)))

        def wait(self, a, b, h):
            self.copy(a, b, h, partner, 0).wait_recv()

        def spread(self, a, h):
            self.far_send(a, 0, h, 1)
            self.far_send(a, 0, h, 3)

        def tile(self, a, b):
            self.on_tile(*self.place(a, b))

        def pass_on(self, a):
            self.wait(a, 3, 0)
            self.far_send(a, 3, 0, 1)
            self.wait(a, 1, 1)
            self.far_send(a, 1, 1, 3)

        def beside(self, a):
            self.wait(a, 3, 1)
            self.tile(a, 3)
            self.wait(a, 1, 0)
            self.tile(a, 1)

        def across(self, a):
            self.wait(a, 2, 0)
            self.wait(a, 2, 1)
            self.tile(a, 2)

        def steps(self):
            for h, step in ((0, 1), (1, 3), (1, 1), (0, 3)):
                self.near_send(0, h, step)
            for h, step in ((0, 1), (1, 3), (1, 1), (0, 3)):
                self.far_send(0, 0, h, step)
            self.tile(0, 0)
            yield
            self.wait(3, 0, 0)
            self.near_send(3, 0, 1)
            self.spread(3, 0)
            yield
            self.wait(1, 0, 1)
            self.near_send(1, 1, 3)
            self.spread(1, 1)
            yield
            self.pass_on(0)
            yield
            self.wait(3, 0, 1)
            self.spread(3, 1)
            self.tile(3, 0)
            yield
            self.wait(1, 0, 0)
            self.spread(1, 0)
            self.tile(1, 0)
            yield
            self.beside(0)
            yield
            self.wait(2, 0, 0)
            self.spread(2, 0)
            self.pass_on(3)
            yield
            self.wait(2, 0, 1)
            self.spread(2, 1)
            self.tile(2, 0)
            self.pass_on(1)
            yield
            self.across(0)
            self.beside(3)
            yield
            self.beside(1)
            yield
            self.pass_on(2)
            yield
            self.across(3)
            self.across(1)
            yield
            self.beside(2)
            self.across(2)

        def run(self):
            for _ in self.steps():
                pass

        def drain(self):
            for copy in self.sent:
                copy.wait_send()

    used = [0]

    def take(count):
        used[0] += count
        return used[0] - count

    class Fan:
        def __init__(self, v, place, out, into):
            self.v, self.place, self.out, self.into = v, place, out, into
            self.base = take(4)

        def copy(self, to):
            return remote(self.out(to), self.into(self.v), ss.at[self.base + to],
                          rs.at[self.base + self.v], device(self.place(to)))

        def send(self, e):
            self.copy((self.v + e) % 4).start()

        def send_to(self, to):
            @pl.when(to != self.v)
            def _():
                self.copy(to).start()

        def wait(self, e):
            source = (self.v + e) % 4
            remote(self.out(self.v), self.into(source), ss.at[self.base],
                   rs.at[self.base + source], partner).wait_recv()

        def drain(self):
            for e in (1, 2, 3):
                self.copy((self.v + e) % 4).wait_send()

        def total(self):
            value = self.out(self.v)[...].astype(F32)
            for e in (1, 3, 2):
                self.wait(e)
                value = value + self.into((self.v + e) % 4)[...].astype(F32)
            return value

    def gather_fan(v, place, buffer):
        return Fan(v, place, lambda to: buffer.at[v], lambda source: buffer.at[source])

    def sum_fan(v, place, out, into):
        return Fan(v, place, lambda to: out.at[to], lambda source: into.at[source])

    pair_base = take(8)

    def to_partner(n, src, dst):
        return remote(src, dst, ss.at[pair_base + n], rs.at[pair_base + n], partner)

    def packed(buffer):
        def at(nn, ff, h):
            return buffer.at[4 * nn + ff, pl.ds(PACKED * h, PACKED), :]

        return at

    def strip(buffer, order):
        def at(nn, ff, h):
            lanes = pl.ds(pl.multiple_of(order(nn, ff) * toks, toks), toks)
            return buffer.at[pl.ds(h * (tile // 2), tile // 2), lanes]

        return at

    a1[:, pl.ds(pl.multiple_of(col * toks, toks), toks)] = acts[...].T
    b1[:, pl.ds(pl.multiple_of(row * toks, toks), toks)] = cot[...].T
    ga = Gather(0, col_axis, strip(a1, lambda nn, ff: 4 * ff + nn))
    gc = Gather(1, row_axis, strip(b1, lambda nn, ff: 4 * nn + ff))
    for _ in itertools.zip_longest(gc.steps(), ga.steps()):
        pass
    if CUT == 1:
        return
    part[...] = lax.dot_general(
        a1[...], b1[...], (((1,), (1,)), ((), ())), preferred_element_type=F32)
    swap = to_partner(0, part, part_in)
    swap.start()
    swap.wait()
    grad = ((part[...] + part_in[...]) * (1.0 / 64.0)).astype(BF16)
    if CUT == 2:
        update[...] = grad
        return

    lines = lax.broadcasted_iota(jnp.int32, (tile, tile), 0)
    places = lax.broadcasted_iota(jnp.int32, (tile, tile), 1)
    identity = jnp.where((lines == places) & (row == col), 1.0, 0.0).astype(F32)
    spots = ((x, at_x), (zl, at_zl), (zh, at_zh), (y, at_y))

    def trace_copy(d, j, spot):
        v, place = spots[d]
        return remote(tr.at[d, spot], tr.at[d, spot], tr_send.at[d, j], tr_recv.at[d, spot],
                      device(place((v + j) % 4)))

    def trace_send(d, value):
        v = spots[d][0]
        tr[d, v] = value
        for j in (1, 2, 3):
            trace_copy(d, j, v).start()

    def trace_wait(d):
        v = spots[d][0]
        for j in (1, 2, 3):
            trace_copy(d, j, (v + j) % 4).wait_recv()
        for j in (1, 2, 3):
            trace_copy(d, j, v).wait_send()
        return (tr[d, 0] + tr[d, 1]) + (tr[d, 2] + tr[d, 3])

    fwd, back = 1 + 2 * g, 3 - 2 * g
    mine = pl.ds(pl.multiple_of(HALF * g, HALF), HALF)
    other = pl.ds(pl.multiple_of(HALF * (1 - g), HALF), HALF)
    own[...] = grad
    ownt[...] = grad.T
    pack(own[mine, :], zt.at[zh])
    ax[x] = zt[zh]
    pack(ownt[mine, :], t_out)

    zs, zr = take(4), take(4)

    def ring_copy(index, step, sem):
        return remote(zt.at[index], zt.at[index], ss.at[zs + sem], rs.at[zr + index],
                      device(at_zh((zh + step) % 4)))

    across = Fan(x, at_x, lambda to: zt.at[to], lambda source: bq.at[4 * y + source])

    def turn(a):
        index = (zh + a) % 4
        across.send_to(index)

        @pl.when(index == x)
        def _():
            bq[4 * y + x] = zt[x]

    def ring_wait(a):
        ring_copy((zh + a) % 4, 1, 0).wait_recv()

    ys, yr, ps = take(16), take(16), take(16)

    def y_copy(b, e, step, sem):
        slot = 4 * ((y + b) % 4) + (x + e) % 4
        return remote(bq.at[slot], bq.at[slot], ss.at[ys + 4 * e + sem], rs.at[yr + slot],
                      device(at_y((y + step) % 4)))

    def hand_over(b):
        place = (y + b) % 4
        four = pl.ds(4 * place, 4)
        return remote(bq.at[four], bp.at[four], ss.at[ps + place], rs.at[ps + place], partner)

    ring = (0, 1, 3, 2)
    acts_fan = gather_fan(x, at_x, ax)
    left_fan = sum_fan(zl, at_zl, lz_out, lz_in)
    right_fan = sum_fan(x, at_x, rx_out, rx_in)
    gt_fan = gather_fan(zl, at_zl, tq)

    def left_group(b):
        place = (y + b) % 4
        hand_over(b).wait_recv()
        acc = jnp.zeros((HALF, tile), F32)
        for e in range(4):
            slot = 4 * place + (x + e) % 4
            unpack(bq.at[slot], gb.at[slot, mine, :])
            unpack(bp.at[slot], gb.at[slot, other, :])
            acc += lax.dot_general(au[(x + e) % 4], gb[slot], (((1,), (1,)), ((), ())),
                                   preferred_element_type=F32)
        pack(acc.astype(BF16), lz_out.at[place])
        left_fan.send_to(place)

    def product(left, fan, out):
        for e in (1, 3, 2, 0):
            index = (x + e) % 4
            acc = jnp.zeros((HALF, tile), F32)
            for k in range(4):
                acc += jnp.dot(left[k], gb[4 * k + index], preferred_element_type=F32)
            pack(acc.astype(BF16), out.at[index])
            if e:
                fan.send(e)

    def trace_step(d):
        trace_send(d, trace_wait(d - 1))

    flip = take(1)
    flip_copy = remote(t_out, tq.at[y], ss.at[flip], rs.at[flip], mirror)

    for step in (1, 3):
        ring_copy(zh, step, step).start()
    turn(0)
    for e in (1, 3, 2):
        acts_fan.send(e)
    wide = grad.astype(F32)
    trace = jnp.sum(wide * wide * (1.0 / D) + 0.9 * (stats[0] * identity))
    trace_send(0, jnp.full((8, 128), trace, F32))
    ring_wait(back)
    ring_copy((zh + back) % 4, fwd, 2).start()
    turn(back)

    ring_wait(fwd)
    turn(fwd)
    trace_step(1)
    ring_wait(2)
    turn(2)
    @pl.when(off)
    def _():
        flip_copy.start()

    @pl.when(jnp.logical_not(off))
    def _():
        tq[zl] = t_out[...]

    for e in ring:
        if e:
            across.wait(e)
        y_copy(0, e, 1, 0).start()
        y_copy(0, e, 3, 1).start()
    hand_over(0).start()
    trace_step(2)
    for e in (1, 3, 2):
        acts_fan.wait(e)
    for k in range(4):
        unpack(ax.at[k], au.at[k])
    for e in ring:
        y_copy(back, e, 1, 0).wait_recv()
        y_copy(back, e, fwd, 2).start()
    hand_over(back).start()
    left_group(0)
    trace_step(3)

    @pl.when(off)
    def _():
        remote(t_out, tq.at[zl], ss.at[flip], rs.at[flip], mirror).wait_recv()

    for e in (1, 3, 2):
        gt_fan.send(e)
    for e in ring:
        y_copy(fwd, e, 1, 0).wait_recv()
    hand_over(fwd).start()
    left_group(back)
    for e in ring:
        y_copy(2, e, 1, 0).wait_recv()
    hand_over(2).start()
    left_group(fwd)
    left_group(2)
    total_trace = trace_wait(3)
    for e in (1, 3, 2):
        gt_fan.wait(e)
    for k in range(4):
        unpack(tq.at[k], tu.at[k])
    product(tu, right_fan, rx_out)
    left_sum = left_fan.total()
    gsum[0] = left_sum
    right_sum = right_fan.total()
    gsum[1] = right_sum
    unpack(gsum.at[g], part.at[mine, :])
    unpack(gsum.at[1 - g], swap_out)
    swap = to_partner(1, swap_out, swap_in)
    swap.start()
    for e in (1, 2, 3):
        across.copy((x + e) % 4).wait_send()
    for sem in (1, 3, 2):
        ring_copy(zh, 1, sem).wait_send()

    @pl.when(off)
    def _():
        flip_copy.wait_send()

    def drain_all():
        for part_done in (ga, gc, acts_fan, left_fan, right_fan, gt_fan):
            part_done.drain()
        for e in range(4):
            for sem in range(3):
                y_copy(0, e, 1, sem).wait_send()
            hand_over(e).wait_send()

    swap.wait()
    part[other, :] = swap_in[...]
    if CUT == 4:
        return
    stat = 0.9 * stats[0] + part[...] * (1.0 / D)
    scale = total_trace[0:1, 0:1] * (1.0 / D)
    root = (jnp.sqrt(lax.rsqrt(scale)) * (5.0 * identity - stat / scale) * 0.25).astype(BF16)
    own[...] = root
    left_root_fan = gather_fan(zl, at_zl, lt)
    side_fan = sum_fan(x, at_x, sx_out, sx_in)

    def unpack_tile(src, dst):
        unpack(src.at[0:PACKED, :], dst.at[0:HALF, :])
        unpack(src.at[PACKED : 2 * PACKED, :], dst.at[HALF : 2 * HALF, :])

    def side_product(between):
        for e in (1, 3, 2):
            left_root_fan.wait(e)
        between()
        for k in range(4):
            unpack(lt.at[k], tu.at[k])
        product(tu, side_fan, sx_out)
        return side_fan.total().astype(BF16)

    slot = 4 * zl + x
    spot = 4 * zh + y
    rb = take(16)

    def give_right(index):
        return remote(rp.at[index], rp.at[index], ss.at[rb + index], rs.at[rb + index], partner)

    @pl.when(g == 0)
    def _():
        pack(own[HALF:, :], t_out)
        give = to_partner(2, t_out, lt.at[zl])
        give.start()
        pack(own[:HALF, :], lt.at[zl])
        for e in (1, 3, 2):
            left_root_fan.send(e)
        new_stats[0] = stat
        roots[0] = root

        def keep(nn, ff):
            @pl.when(4 * nn + ff != spot)
            def _():
                give_right(4 * nn + ff).start()

        rights = Gather(2, row_axis, packed(rp), keep)
        steps = rights.steps()

        def between():
            to_partner(5, rp.at[spot], rp.at[spot]).wait_recv()
            next(steps)

        zt[0] = side_product(between)
        side = to_partner(3, zt.at[0], sp.at[slot, pl.ds(0, PACKED), :])
        side.start()
        for _ in steps:
            pass
        left_root_fan.drain()
        side_fan.drain()
        rights.drain()
        give.wait_send()
        side.wait_send()
        for k in range(1, 16):
            give_right((spot + k) % 16).wait_send()
        drain_all()
        to_partner(4, up_in, up_in).wait_recv()
        update[...] = up_in[...]

    @pl.when(g == 1)
    def _():
        pack(own[:HALF, :], rp.at[spot, 0:PACKED, :])
        pack(own[HALF:, :], rp.at[spot, PACKED : 2 * PACKED, :])
        give = to_partner(5, rp.at[spot], rp.at[spot])
        give.start()
        to_partner(2, t_out, lt.at[zl]).wait_recv()
        for e in (1, 3, 2):
            left_root_fan.send(e)
        new_stats[0] = stat
        roots[0] = root
        sp[slot, PACKED : 2 * PACKED, :] = side_product(lambda: None)
        part[...] = jnp.zeros_like(part)
        to_partner(3, zt.at[0], sp.at[slot, pl.ds(0, PACKED), :]).wait_recv()
        early, late = [], []

        def update_term(nn, ff):
            index = 4 * ff + nn

            @pl.when(index != spot)
            def _():
                give_right(index).wait_recv()

            unpack_tile(sp.at[4 * nn + ff], tmp)
            unpack_tile(rp.at[index], panel)
            part[...] += jnp.dot(tmp[...], panel[...], preferred_element_type=F32)

        def arrived(nn, ff):
            if late:
                update_term(nn, ff)
            else:
                early.append((nn, ff))

        gather = Gather(3, col_axis, packed(sp), arrived)
        for k, _ in enumerate(gather.steps()):
            if k == 8:
                late.append(k)
                for nn, ff in early:
                    update_term(nn, ff)
        result = part[...].astype(BF16)
        update[...] = result
        own[...] = result
        final = to_partner(4, own, up_in)
        final.start()
        give.wait_send()
        left_root_fan.drain()
        side_fan.drain()
        gather.drain()
        drain_all()
        final.wait_send()


def shards(activations, cotangent, statistics):
    toks, tile = activations.shape
    vmem = pl.BlockSpec(memory_space=pltpu.VMEM)
    half = (PACKED, MAIN)
    quad, many = pltpu.VMEM((4,) + half, BF16), pltpu.VMEM((16,) + half, BF16)
    pairs = pltpu.VMEM((16, 2 * PACKED, MAIN), BF16)
    strips = pltpu.VMEM((tile, 16 * toks), BF16)
    whole = pltpu.VMEM((tile, tile), BF16)
    halves = pltpu.VMEM((4, HALF, tile), BF16)
    return pl.pallas_call(
        kernel,
        out_shape=(
            jax.ShapeDtypeStruct((1, tile, tile), F32),
            jax.ShapeDtypeStruct((1, tile, tile), BF16),
            jax.ShapeDtypeStruct((tile, tile), BF16),
        ),
        in_specs=[vmem] * 3,
        out_specs=(vmem,) * 3,
        scratch_shapes=[
            strips, strips, whole, whole, quad, many, many, pltpu.VMEM((16, tile, tile), BF16),
            quad, halves, quad, halves, pltpu.VMEM(half, BF16), quad, quad, quad, quad,
            pltpu.VMEM((HALF, tile), F32), pltpu.VMEM((HALF, tile), F32),
            pltpu.VMEM((tile, tile), F32), pltpu.VMEM((tile, tile), F32),
            pltpu.VMEM((2,) + half, F32), quad, quad, quad, pairs, pairs,
            whole, whole, whole, pltpu.VMEM((4, 4, 8, 128), F32),
            pltpu.SemaphoreType.DMA((4, 30)),
            pltpu.SemaphoreType.DMA((4, 32)),
            pltpu.SemaphoreType.DMA((112,)),
            pltpu.SemaphoreType.DMA((112,)),
            pltpu.SemaphoreType.DMA((4, 4)),
            pltpu.SemaphoreType.DMA((4, 4)),
        ],
        compiler_params=pltpu.CompilerParams(
            collective_id=0, has_side_effects=True, vmem_limit_bytes=48 * 2**20
        ),
        cost_estimate=pl.CostEstimate(flops=3 * 10**9, bytes_accessed=2 * 10**6, transcendentals=0),
    )(activations, cotangent, statistics)


def solution(mesh):
    placed = (P(("group", "col"), "row"), P(("group", "row"), "col"), P("group", "row", "col"))
    return jax.shard_map(
        shards,
        mesh=mesh,
        in_specs=placed,
        out_specs=(P("group", "row", "col"), P("group", "row", "col"), P("row", "col")),
        check_vma=False,
    )
```
